32 devices in a mesh: light: 4 (over y, core), view: 8 (over z, x).
Axes of the slice: x: 2, y: 2, z: 4, core: 2. Of those that a mesh axis runs over, the one named last changes fastest.
Arguments:
- density: float32 [128, 32, 4096], P('light', 'view'), may hold values from 0.1 to 8
- emission: float32 [128, 32, 4096], P('light', 'view'), may hold values from 0.1 to 1
- facing: int32 [128], P('light'), may hold values 0 or 1
Outputs:
- radiance: float32 [128, 4096], P('light', 'view')
- coverage: float32 [128, 4096], P('light', 'view')
The draws below stay inside these ranges and needn't reach their ends.
All inputs are finite; a program needn't handle non-finite values. No bound on the sum of `facing` on one device may be relied on, other than what follows from the above.
Results may differ from the reference program's by a relative error of at most 0.0003.
Values sent between devices are 32-bit elements; how exact they have to be, the bound alone decides.
A program may use at most 64 MiB of HBM per device.

```python
import math
import jax
import jax.numpy as jnp
from jax import lax

NP = 4096
NL = 128
NV = 32


def set_ends(array, key, smallest, top_value):
    extent = array.shape
    index_at = [jax.random.randint(jax.random.fold_in(key, axis), (), 0, extent[axis]) for axis in range(len(extent))]
    array = array.at[tuple(index_at)].set(smallest)
    longest = extent.index(max(extent))
    index_at[longest] = (index_at[longest] + 1) % extent[longest]
    return array.at[tuple(index_at)].set(top_value)


def levels(key, extent, split, least, top_value):
    level, own = 1.0, jax.random.fold_in(key, 6)
    for axis_at, parts in split:
        heights = jnp.exp(jax.random.uniform(jax.random.fold_in(own, axis_at), (parts,), jnp.float32, least / len(split), top_value / len(split)))
        level = level * jnp.repeat(heights, extent[axis_at] // parts).reshape([-1 if axis == axis_at else 1 for axis in range(len(extent))])
    return level


def setup_inputs(seed: int = 0) -> dict:
    splits = jax.random.split(jax.random.key(seed), 4)
    density = jnp.clip(jnp.exp(math.log(8.0) - 4.3820266 * jax.random.uniform(splits[0], (NL, NV, NP), jnp.float32) ** levels(splits[0], (NL, NV, NP), ((0, 4), (1, 8)), -0.2, 0.2)), 0.1, 8.0)
    emission = jnp.clip(0.1 + 0.9 * jax.random.uniform(splits[1], (NL, NV, NP), jnp.float32) ** levels(splits[1], (NL, NV, NP), ((0, 4), (1, 8)), -0.2, 0.2), 0.1, 1.0)
    facing = set_ends((jax.random.randint(splits[2], (NL,), 0, 2) < 1).astype(jnp.int32), jax.random.fold_in(splits[2], 1), 0, 1)
    return {"density": density, "emission": emission, "facing": facing}


def render_block(dens, emit, facing):
    nl = dens.shape[0]
    nv = dens.shape[1]
    tau_light = dens * (1.0 / nl)
    tau_view = dens * (1.0 / nv)
    depth = jnp.cumsum(tau_light, axis=0) - tau_light
    lit = emit * (0.2 + jnp.exp(-depth)) * (1.0 - jnp.exp(-tau_view))
    running = jnp.cumsum(tau_view, axis=1)
    before = running - tau_view
    total = jnp.sum(tau_view, axis=1)
    after = total[:, None, :] - running
    forward = jnp.sum(lit * jnp.exp(-before), axis=1)
    backward = jnp.sum(lit * jnp.exp(-after), axis=1)
    image = jnp.where((facing == 1)[:, None], backward, forward)
    return image, jnp.exp(-total)


def reference(density, emission, facing):
    nl, nv, npix = density.shape
    width = math.gcd(npix, 128)
    count = npix // width

    def one(index):
        start = (index * width).astype(jnp.int32)
        dens = lax.dynamic_slice_in_dim(density, start, width, 2)
        emit = lax.dynamic_slice_in_dim(emission, start, width, 2)
        return render_block(dens, emit, facing)

    images, covers = lax.map(one, jnp.arange(count, dtype=jnp.int32))
    radiance = jnp.moveaxis(images, 0, 1).reshape(nl, npix)
    coverage = jnp.moveaxis(covers, 0, 1).reshape(nl, npix)
    return radiance, coverage
```

```python
import functools

import jax
import jax.numpy as jnp
from jax import lax
from jax.experimental import pallas as pl
from jax.experimental.pallas import tpu as pltpu
from jax.sharding import PartitionSpec as P

LANES = 128
SUB = 8
CHUNKS = 4
MESH = pl.DeviceIdType.MESH


def transposed(regs, width, block):
    regs, bit = list(regs), 1
    while bit < len(regs):
        low = (block & bit) == 0
        for i in range(len(regs)):
            if i & bit == 0:
                a, b = regs[i], regs[i | bit]
                regs[i] = jnp.where(low, a, pltpu.roll(b, bit * width, 0))
                regs[i | bit] = jnp.where(low, pltpu.roll(a, SUB - bit * width, 0), b)
        bit *= 2
    return regs


def kernel(
    rows, cells, columns, lights, views,
    facing, dens_hbm, emis_hbm, radiance, coverage,
    dens, emis, slab, slabs, incoming, msg, xbuf, comb, zbuf,
    load_sem, light_send, light_recv, x_send, x_recv, z_send, z_recv,
):
    light, view = lax.axis_index("light"), lax.axis_index("view")
    x, z = lax.rem(view, 2), lax.div(view, 2)
    deep = views // 2
    tiles = columns // (SUB * LANES)
    width = columns // (views * LANES)
    n = SUB // width
    groups = rows // n
    light_scale = 1.0 / (rows * lights)
    view_scale = 1.0 / (cells * views)
    power = (rows * lights) // (cells * views)
    whole_power = power * cells * views == rows * lights
    pitch = columns // LANES * cells
    part = rows * pitch // CHUNKS
    per_chunk = groups // CHUNKS
    order = list(range(1, deep)) + [0]

    loads = [
        [
            pltpu.make_async_copy(
                source.at[pl.ds(k * part, part)], target.at[pl.ds(k * part, part)], load_sem.at[t, k]
            )
            for k in range(CHUNKS)
        ]
        for t, (source, target) in enumerate(((dens_hbm, dens), (emis_hbm, emis)))
    ]
    for copy in loads[0] + loads[1]:
        copy.start()

    barrier = pltpu.get_barrier_semaphore()
    for d in range(1, lights):
        pl.semaphore_signal(
            barrier, inc=1, device_id={"light": lax.rem(light + d, lights)}, device_id_type=MESH
        )
    pl.semaphore_signal(barrier, inc=1, device_id={"view": view + 1 - 2 * x}, device_id_type=MESH)
    for q in range(1, deep):
        pl.semaphore_signal(
            barrier, inc=1, device_id={"view": lax.rem(z + q, deep) * 2 + x}, device_id_type=MESH
        )

    block = lax.broadcasted_iota(jnp.int32, (SUB, LANES), 0) // width

    def tile(ref, row, m, v):
        return ref[pl.ds(row * pitch + m * SUB * cells + v, SUB, stride=cells), :]

    def turned(g):
        mask = jnp.full((SUB, LANES), facing[g * n], jnp.int32)
        for i in range(1, n):
            mask = jnp.where(block == i, facing[g * n + i], mask)
        return mask

    def first(g, sums):
        sums = list(sums)
        for m in range(tiles):
            totals = []
            for i in range(n):
                total = None
                for v in range(cells):
                    d = tile(dens, g * n + i, m, v)
                    sums[m * cells + v] = sums[m * cells + v] + d
                    total = d if total is None else total + d
                totals.append(jnp.exp(total * -view_scale))
            for o, packed in enumerate(transposed(totals, width, block)):
                msg[0, m * n + o, g] = packed
        return tuple(sums)

    sums = tuple(jnp.zeros((SUB, LANES), jnp.float32) for _ in range(tiles * cells))
    for k in range(CHUNKS):
        loads[0][k].wait()
        sums = lax.fori_loop(k * per_chunk, (k + 1) * per_chunk, first, sums)
    for j in range(tiles * cells):
        slab[j] = sums[j]

    pl.semaphore_wait(barrier, lights - 1 + 1 + deep - 1)

    def to_light(d):
        return pltpu.make_async_remote_copy(
            src_ref=slab,
            dst_ref=slabs.at[d - 1],
            send_sem=light_send.at[d - 1],
            recv_sem=light_recv.at[d - 1],
            device_id={"light": lax.rem(light + d, lights)},
            device_id_type=MESH,
        )

    def to_x(t, q):
        owner = lax.rem(z + q, deep) * 2
        return pltpu.make_async_remote_copy(
            src_ref=msg.at[t, owner + 1 - x],
            dst_ref=xbuf.at[t, q],
            send_sem=x_send.at[t, q],
            recv_sem=x_recv.at[t, q],
            device_id={"view": view + 1 - 2 * x},
            device_id_type=MESH,
        )

    def to_z(t, q):
        return pltpu.make_async_remote_copy(
            src_ref=comb.at[t, q - 1],
            dst_ref=zbuf.at[t, q],
            send_sem=z_send.at[t, q],
            recv_sem=z_recv.at[t, q],
            device_id={"view": lax.rem(z + q, deep) * 2 + x},
            device_id_type=MESH,
        )

    for d in reversed(range(1, lights)):
        @pl.when(light + d < lights)
        def _():
            to_light(d).start()
    for q in order:
        to_x(0, q).start()

    def join_trans(q):
        owner = lax.rem(z + q, deep) * 2 + x
        to_x(0, q).wait_recv()

        def step(g, carry):
            value = msg[0, owner, g] * xbuf[0, q, g]
            if q:
                comb[0, q - 1, g] = value
            else:
                zbuf[0, 0, g] = value
            return carry

        lax.fori_loop(0, groups, step, 0)
        if q:
            to_z(0, q).start()

    def join_color(q):
        owner = lax.rem(z + q, deep) * 2 + x
        to_x(1, q).wait_recv()

        def step(g, carry):
            mine, other = msg[1, owner, g], xbuf[1, q, g]
            value = jnp.where(
                turned(g) == x, mine + msg[0, owner, g] * other, other + xbuf[0, q, g] * mine
            )
            if q:
                comb[1, q - 1, g] = value
            else:
                zbuf[1, 0, g] = value
            return carry

        lax.fori_loop(0, groups, step, 0)
        if q:
            to_z(1, q).start()

    early = deep // 2
    for q in order[:early]:
        join_trans(q)

    incoming[...] = jnp.zeros_like(incoming)
    for d in range(1, lights):
        @pl.when(light >= d)
        def _():
            to_light(d).wait_recv()
            incoming[...] += slabs[d - 1]

    def second(g, lights_in):
        lights_in = list(lights_in)
        swap = [facing[g * n + i] == 1 for i in range(n)]
        for m in range(tiles):
            colors = []
            for i in range(n):
                lit, through = [], []
                for v in range(cells):
                    d = tile(dens, g * n + i, m, v)
                    thin = jnp.exp(d * -light_scale)
                    passed = lax.integer_pow(thin, power) if whole_power else jnp.exp(d * -view_scale)
                    reach = lights_in[m * cells + v]
                    lit.append(tile(emis, g * n + i, m, v) * (0.2 + reach) * (1.0 - passed))
                    through.append(passed)
                    lights_in[m * cells + v] = reach * thin
                forward, backward = lit[-1], lit[0]
                for v in range(cells - 2, -1, -1):
                    forward = lit[v] + through[v] * forward
                for v in range(1, cells):
                    backward = lit[v] + through[v] * backward
                colors.append(jnp.where(swap[i], backward, forward))
            for o, packed in enumerate(transposed(colors, width, block)):
                msg[1, m * n + o, g] = packed
        return tuple(lights_in)

    lights_in = tuple(jnp.exp(incoming[j] * -light_scale) for j in range(tiles * cells))
    for k in range(CHUNKS):
        loads[1][k].wait()
        lights_in = lax.fori_loop(k * per_chunk, (k + 1) * per_chunk, second, lights_in)
    for q in order:
        to_x(1, q).start()

    for q in order[early:]:
        join_trans(q)
    for q in order:
        join_color(q)
    for q in range(1, deep):
        for t in range(2):
            to_z(t, q).wait_recv()

    def last(g, carry):
        color = [None] * deep
        trans = [None] * deep
        for at in range(deep):
            slot = lax.rem(z + deep - at, deep)
            trans[at], color[at] = zbuf[0, slot, g], zbuf[1, slot, g]
        forward, backward, total = color[-1], color[0], trans[0]
        for at in range(deep - 2, -1, -1):
            forward = color[at] + trans[at] * forward
        for at in range(1, deep):
            backward = color[at] + trans[at] * backward
            total = total * trans[at]
        radiance[g] = jnp.where(turned(g) == 1, backward, forward)
        coverage[g] = total
        return carry

    lax.fori_loop(0, groups, last, 0)

    for d in range(1, lights):
        @pl.when(light + d < lights)
        def _():
            to_light(d).wait_send()
    for t in range(2):
        for q in range(deep):
            to_x(t, q).wait_send()
            if q:
                to_z(t, q).wait_send()


def shards(density, emission, facing):
    rows, cells, columns = density.shape
    lights, views = lax.axis_size("light"), lax.axis_size("view")
    deep = views // 2
    width = columns // (views * LANES)
    groups = rows * width // SUB
    tiles = columns // (SUB * LANES)

    def linear(a):
        a = a.reshape(rows, cells, columns // LANES, LANES)
        return a.transpose(0, 2, 1, 3).reshape(-1, LANES)

    f32 = jnp.float32
    piece = (groups, SUB, LANES)
    lines = rows * cells * columns // LANES
    radiance, coverage = pl.pallas_call(
        functools.partial(kernel, rows, cells, columns, lights, views),
        out_shape=[jax.ShapeDtypeStruct(piece, f32)] * 2,
        in_specs=[
            pl.BlockSpec(memory_space=pltpu.SMEM),
            pl.BlockSpec(memory_space=pltpu.HBM),
            pl.BlockSpec(memory_space=pltpu.HBM),
        ],
        out_specs=[pl.BlockSpec(memory_space=pltpu.VMEM)] * 2,
        scratch_shapes=[
            pltpu.VMEM((lines, LANES), f32),
            pltpu.VMEM((lines, LANES), f32),
            pltpu.VMEM((tiles * cells, SUB, LANES), f32),
            pltpu.VMEM((lights - 1, tiles * cells, SUB, LANES), f32),
            pltpu.VMEM((tiles * cells, SUB, LANES), f32),
            pltpu.VMEM((2, views) + piece, f32),
            pltpu.VMEM((2, deep) + piece, f32),
            pltpu.VMEM((2, deep - 1) + piece, f32),
            pltpu.VMEM((2, deep) + piece, f32),
            pltpu.SemaphoreType.DMA((2, CHUNKS)),
            pltpu.SemaphoreType.DMA((lights - 1,)),
            pltpu.SemaphoreType.DMA((lights - 1,)),
            pltpu.SemaphoreType.DMA((2, deep)),
            pltpu.SemaphoreType.DMA((2, deep)),
            pltpu.SemaphoreType.DMA((2, deep)),
            pltpu.SemaphoreType.DMA((2, deep)),
        ],
        compiler_params=pltpu.CompilerParams(
            collective_id=0, has_side_effects=True, vmem_limit_bytes=48 * 2**20
        ),
    )(facing, linear(density), linear(emission))
    return radiance.reshape(rows, width * LANES), coverage.reshape(rows, width * LANES)


def solution(mesh):
    return jax.shard_map(
        shards,
        mesh=mesh,
        in_specs=(P("light", "view", None), P("light", "view", None), P("light")),
        out_specs=(P("light", "view"), P("light", "view")),
        check_vma=False,
    )
```

```python
import functools

import jax
import jax.numpy as jnp
from jax import lax
from jax.experimental import pallas as pl
from jax.experimental.pallas import tpu as pltpu
from jax.sharding import PartitionSpec as P

LANES = 128
SUB = 8
MESH = pl.DeviceIdType.MESH


def transposed(regs, width, block):
    regs, bit = list(regs), 1
    while bit < len(regs):
        low = (block & bit) == 0
        for i in range(len(regs)):
            if i & bit == 0:
                a, b = regs[i], regs[i | bit]
                regs[i] = jnp.where(low, a, pltpu.roll(b, bit * width, 0))
                regs[i | bit] = jnp.where(low, pltpu.roll(a, SUB - bit * width, 0), b)
        bit *= 2
    return regs


def kernel(
    rows, cells, columns, lights, views,
    facing, dens_hbm, emis_hbm, radiance, coverage,
    dens, emis, slab, slabs, incoming, msg, xbuf, comb, zbuf,
    load_sem, light_send, light_recv, x_send, x_recv, z_send, z_recv,
):
    light, view = lax.axis_index("light"), lax.axis_index("view")
    x, z = lax.rem(view, 2), lax.div(view, 2)
    deep = views // 2
    tiles = columns // (SUB * LANES)
    width = columns // (views * LANES)
    n = SUB // width
    groups = rows // n
    light_scale = 1.0 / (rows * lights)
    view_scale = 1.0 / (cells * views)
    power = (rows * lights) // (cells * views)
    whole_power = power * cells * views == rows * lights
    lines = SUB * cells
    per_tile = deep // tiles
    order = list(range(1, deep)) + [0]
    first_tile = lax.div(z, per_tile)
    visits = [lax.rem(first_tile + k, tiles) for k in list(range(1, tiles)) + [0]]

    loads = [
        [
            pltpu.make_async_copy(
                source.at[:, pl.ds(pl.multiple_of(m * lines, SUB), lines), :], target.at[k], load_sem.at[t, k]
            )
            for k, m in enumerate(visits)
        ]
        for t, (source, target) in enumerate(((dens_hbm, dens), (emis_hbm, emis)))
    ]
    for copy in loads[0] + loads[1]:
        copy.start()

    barrier = pltpu.get_barrier_semaphore()
    for d in range(1, lights):
        pl.semaphore_signal(
            barrier, inc=1, device_id={"light": lax.rem(light + d, lights)}, device_id_type=MESH
        )
    pl.semaphore_signal(barrier, inc=1, device_id={"view": view + 1 - 2 * x}, device_id_type=MESH)
    for q in range(1, deep):
        pl.semaphore_signal(
            barrier, inc=1, device_id={"view": lax.rem(z + q, deep) * 2 + x}, device_id_type=MESH
        )

    block = lax.broadcasted_iota(jnp.int32, (SUB, LANES), 0) // width

    def tile(ref, k, row, v):
        return ref[k, row, pl.ds(v, SUB, stride=cells), :]

    def turned(g):
        mask = jnp.full((SUB, LANES), facing[g * n], jnp.int32)
        for i in range(1, n):
            mask = jnp.where(block == i, facing[g * n + i], mask)
        return mask

    def first(k, m, g, sums):
        sums, totals = list(sums), []
        for i in range(n):
            total = None
            for v in range(cells):
                d = tile(dens, k, g * n + i, v)
                sums[v] = sums[v] + d
                total = d if total is None else total + d
            totals.append(jnp.exp(total * -view_scale))
        for o, packed in enumerate(transposed(totals, width, block)):
            msg[0, m * n + o, g] = packed
        return tuple(sums)

    def to_light(d, k):
        return pltpu.make_async_remote_copy(
            src_ref=slab.at[k],
            dst_ref=slabs.at[d - 1, k],
            send_sem=light_send.at[d - 1, k],
            recv_sem=light_recv.at[d - 1, k],
            device_id={"light": lax.rem(light + d, lights)},
            device_id_type=MESH,
        )

    def to_x(t, q):
        owner = lax.rem(z + q, deep) * 2
        return pltpu.make_async_remote_copy(
            src_ref=msg.at[t, owner + 1 - x],
            dst_ref=xbuf.at[t, q],
            send_sem=x_send.at[t, q],
            recv_sem=x_recv.at[t, q],
            device_id={"view": view + 1 - 2 * x},
            device_id_type=MESH,
        )

    def to_z(t, q):
        return pltpu.make_async_remote_copy(
            src_ref=comb.at[t, q - 1],
            dst_ref=zbuf.at[t, q],
            send_sem=z_send.at[t, q],
            recv_sem=z_recv.at[t, q],
            device_id={"view": lax.rem(z + q, deep) * 2 + x},
            device_id_type=MESH,
        )

    def send_x(t, m):
        for i in list(range(1, per_tile)) + [0]:
            to_x(t, lax.rem(m * per_tile + i - z + deep, deep)).start()

    zeros = tuple(jnp.zeros((SUB, LANES), jnp.float32) for _ in range(cells))
    for k, m in enumerate(visits):
        loads[0][k].wait()
        sums = lax.fori_loop(0, groups, functools.partial(first, k, m), zeros, unroll=2)
        for v in range(cells):
            slab[k, v] = sums[v]
        if k == 0:
            pl.semaphore_wait(barrier, lights - 1 + 1 + deep - 1)
        for d in reversed(range(1, lights)):
            @pl.when(light + d < lights)
            def _():
                to_light(d, k).start()
        send_x(0, m)

    def join_trans(q):
        owner = lax.rem(z + q, deep) * 2 + x
        to_x(0, q).wait_recv()

        def step(g, carry):
            value = msg[0, owner, g] * xbuf[0, q, g]
            if q:
                comb[0, q - 1, g] = value
            else:
                zbuf[0, 0, g] = value
            return carry

        lax.fori_loop(0, groups, step, 0, unroll=min(4, groups))
        if q:
            to_z(0, q).start()

    def join_color(q):
        owner = lax.rem(z + q, deep) * 2 + x
        to_x(1, q).wait_recv()

        def step(g, carry):
            mine, other = msg[1, owner, g], xbuf[1, q, g]
            value = jnp.where(
                turned(g) == x, mine + msg[0, owner, g] * other, other + xbuf[0, q, g] * mine
            )
            if q:
                comb[1, q - 1, g] = value
            else:
                zbuf[1, 0, g] = value
            return carry

        lax.fori_loop(0, groups, step, 0, unroll=min(4, groups))
        if q:
            to_z(1, q).start()

    def second(k, m, g, lights_in):
        lights_in, colors = list(lights_in), []
        for i in range(n):
            lit, through = [], []
            for v in range(cells):
                d = tile(dens, k, g * n + i, v)
                thin = jnp.exp(d * -light_scale)
                passed = lax.integer_pow(thin, power) if whole_power else jnp.exp(d * -view_scale)
                lit.append(tile(emis, k, g * n + i, v) * (0.2 + lights_in[v]) * (1.0 - passed))
                through.append(passed)
                lights_in[v] = lights_in[v] * thin
            forward, backward = lit[-1], lit[0]
            for v in range(cells - 2, -1, -1):
                forward = lit[v] + through[v] * forward
            for v in range(1, cells):
                backward = lit[v] + through[v] * backward
            colors.append(jnp.where(facing[g * n + i] == 1, backward, forward))
        for o, packed in enumerate(transposed(colors, width, block)):
            msg[1, m * n + o, g] = packed
        return tuple(lights_in)

    incoming[...] = jnp.zeros_like(incoming)
    for k, m in enumerate(visits):
        for d in range(1, lights):
            @pl.when(light >= d)
            def _():
                to_light(d, k).wait_recv()
                incoming[k] += slabs[d - 1, k]
        loads[1][k].wait()
        lights_in = tuple(jnp.exp(incoming[k, v] * -light_scale) for v in range(cells))
        lax.fori_loop(0, groups, functools.partial(second, k, m), lights_in, unroll=2)
        send_x(1, m)
        for q in order[k * per_tile : (k + 1) * per_tile]:
            join_trans(q)
    for q in order:
        join_color(q)
    for q in range(1, deep):
        for t in range(2):
            to_z(t, q).wait_recv()

    def last(g, carry):
        color = [None] * deep
        trans = [None] * deep
        for at in range(deep):
            slot = lax.rem(z + deep - at, deep)
            trans[at], color[at] = zbuf[0, slot, g], zbuf[1, slot, g]
        forward, backward, total = color[-1], color[0], trans[0]
        for at in range(deep - 2, -1, -1):
            forward = color[at] + trans[at] * forward
        for at in range(1, deep):
            backward = color[at] + trans[at] * backward
            total = total * trans[at]
        radiance[g] = jnp.where(turned(g) == 1, backward, forward)
        coverage[g] = total
        return carry

    lax.fori_loop(0, groups, last, 0, unroll=2)

    for d in range(1, lights):
        @pl.when(light + d < lights)
        def _():
            for k in range(tiles):
                to_light(d, k).wait_send()
    for t in range(2):
        for q in range(deep):
            to_x(t, q).wait_send()
            if q:
                to_z(t, q).wait_send()


def shards(density, emission, facing):
    rows, cells, columns = density.shape
    lights, views = lax.axis_size("light"), lax.axis_size("view")
    deep = views // 2
    width = columns // (views * LANES)
    groups = rows * width // SUB
    tiles = columns // (SUB * LANES)

    def linear(a):
        a = a.reshape(rows, cells, columns // LANES, LANES)
        return a.transpose(0, 2, 1, 3).reshape(rows, -1, LANES)

    f32 = jnp.float32
    piece = (groups, SUB, LANES)
    field = (tiles, rows, SUB * cells, LANES)
    radiance, coverage = pl.pallas_call(
        functools.partial(kernel, rows, cells, columns, lights, views),
        out_shape=[jax.ShapeDtypeStruct(piece, f32)] * 2,
        in_specs=[
            pl.BlockSpec(memory_space=pltpu.SMEM),
            pl.BlockSpec(memory_space=pltpu.HBM),
            pl.BlockSpec(memory_space=pltpu.HBM),
        ],
        out_specs=[pl.BlockSpec(memory_space=pltpu.VMEM)] * 2,
        scratch_shapes=[
            pltpu.VMEM(field, f32),
            pltpu.VMEM(field, f32),
            pltpu.VMEM((tiles, cells, SUB, LANES), f32),
            pltpu.VMEM((lights - 1, tiles, cells, SUB, LANES), f32),
            pltpu.VMEM((tiles, cells, SUB, LANES), f32),
            pltpu.VMEM((2, views) + piece, f32),
            pltpu.VMEM((2, deep) + piece, f32),
            pltpu.VMEM((2, deep - 1) + piece, f32),
            pltpu.VMEM((2, deep) + piece, f32),
            pltpu.SemaphoreType.DMA((2, tiles)),
            pltpu.SemaphoreType.DMA((lights - 1, tiles)),
            pltpu.SemaphoreType.DMA((lights - 1, tiles)),
            pltpu.SemaphoreType.DMA((2, deep)),
            pltpu.SemaphoreType.DMA((2, deep)),
            pltpu.SemaphoreType.DMA((2, deep)),
            pltpu.SemaphoreType.DMA((2, deep)),
        ],
        compiler_params=pltpu.CompilerParams(
            collective_id=0, has_side_effects=True, vmem_limit_bytes=62 * 2**20
        ),
    )(facing, linear(density), linear(emission))
    return radiance.reshape(rows, width * LANES), coverage.reshape(rows, width * LANES)


def solution(mesh):
    return jax.shard_map(
        shards,
        mesh=mesh,
        in_specs=(P("light", "view", None), P("light", "view", None), P("light")),
        out_specs=(P("light", "view"), P("light", "view")),
        check_vma=False,
    )
```

```python
import functools

import jax
import jax.numpy as jnp
from jax import lax
from jax.experimental import pallas as pl
from jax.experimental.pallas import tpu as pltpu
from jax.sharding import PartitionSpec as P

LANES = 128
SUB = 8
MESH = pl.DeviceIdType.MESH


def transposed(regs, width, block):
    regs, bit = list(regs), 1
    while bit < len(regs):
        low = (block & bit) == 0
        for i in range(len(regs)):
            if i & bit == 0:
                a, b = regs[i], regs[i | bit]
                regs[i] = jnp.where(low, a, pltpu.roll(b, bit * width, 0))
                regs[i | bit] = jnp.where(low, pltpu.roll(a, SUB - bit * width, 0), b)
        bit *= 2
    return regs


def kernel(
    rows, cells, columns, lights, views,
    facing, dens_hbm, emis_hbm, radiance, coverage,
    dens, emis, slab, slabs, incoming, msg, xbuf, comb, zbuf,
    load_sem, light_send, light_recv, x_send, x_recv, z_send, z_recv,
):
    light, view = lax.axis_index("light"), lax.axis_index("view")
    x, z = lax.rem(view, 2), lax.div(view, 2)
    deep = views // 2
    tiles = columns // (SUB * LANES)
    width = columns // (views * LANES)
    n = SUB // width
    groups = rows // n
    light_scale = 1.0 / (rows * lights)
    view_scale = 1.0 / (cells * views)
    power = (rows * lights) // (cells * views)
    whole_power = power * cells * views == rows * lights
    lines = SUB * cells
    per_tile = deep // tiles
    order = list(range(1, deep)) + [0]
    first_tile = lax.div(z, per_tile)
    visits = [lax.rem(first_tile + k, tiles) for k in list(range(1, tiles)) + [0]]

    loads = [
        [
            pltpu.make_async_copy(
                source.at[:, pl.ds(pl.multiple_of(m * lines, SUB), lines), :], target.at[k], load_sem.at[t, k]
            )
            for k, m in enumerate(visits)
        ]
        for t, (source, target) in enumerate(((dens_hbm, dens), (emis_hbm, emis)))
    ]
    for copy in loads[0] + loads[1]:
        copy.start()

    barrier = pltpu.get_barrier_semaphore()
    for d in range(1, lights):
        pl.semaphore_signal(
            barrier, inc=1, device_id={"light": lax.rem(light + d, lights)}, device_id_type=MESH
        )
    pl.semaphore_signal(barrier, inc=1, device_id={"view": view + 1 - 2 * x}, device_id_type=MESH)
    for q in range(1, deep):
        pl.semaphore_signal(
            barrier, inc=1, device_id={"view": lax.rem(z + q, deep) * 2 + x}, device_id_type=MESH
        )

    block = lax.broadcasted_iota(jnp.int32, (SUB, LANES), 0) // width

    def tile(ref, k, row, v):
        return ref[k, row, pl.ds(v, SUB, stride=cells), :]

    def turned(g):
        mask = jnp.full((SUB, LANES), facing[g * n], jnp.int32)
        for i in range(1, n):
            mask = jnp.where(block == i, facing[g * n + i], mask)
        return mask

    def first(k, m, g, sums):
        sums, totals = list(sums), []
        for i in range(n):
            total = None
            for v in range(cells):
                d = tile(dens, k, g * n + i, v)
                sums[v] = sums[v] + d
                total = d if total is None else total + d
            totals.append(jnp.exp(total * -view_scale))
        for o, packed in enumerate(transposed(totals, width, block)):
            msg[0, m * n + o, g] = packed
        return tuple(sums)

    def to_light(d, k):
        return pltpu.make_async_remote_copy(
            src_ref=slab.at[k],
            dst_ref=slabs.at[d - 1, k],
            send_sem=light_send.at[d - 1, k],
            recv_sem=light_recv.at[d - 1, k],
            device_id={"light": lax.rem(light + d, lights)},
            device_id_type=MESH,
        )

    def to_x(t, q):
        owner = lax.rem(z + q, deep) * 2
        return pltpu.make_async_remote_copy(
            src_ref=msg.at[t, owner + 1 - x],
            dst_ref=xbuf.at[t, q],
            send_sem=x_send.at[t, q],
            recv_sem=x_recv.at[t, q],
            device_id={"view": view + 1 - 2 * x},
            device_id_type=MESH,
        )

    def to_z(t, q):
        return pltpu.make_async_remote_copy(
            src_ref=comb.at[t, q - 1],
            dst_ref=zbuf.at[t, q],
            send_sem=z_send.at[t, q],
            recv_sem=z_recv.at[t, q],
            device_id={"view": lax.rem(z + q, deep) * 2 + x},
            device_id_type=MESH,
        )

    def send_x(t, m):
        for i in list(range(1, per_tile)) + [0]:
            to_x(t, lax.rem(m * per_tile + i - z + deep, deep)).start()

    zeros = tuple(jnp.zeros((SUB, LANES), jnp.float32) for _ in range(cells))
    for k, m in enumerate(visits):
        loads[0][k].wait()
        sums = lax.fori_loop(0, groups, functools.partial(first, k, m), zeros, unroll=2)
        for v in range(cells):
            slab[k, v] = sums[v]
        if k == 0:
            pl.semaphore_wait(barrier, lights - 1 + 1 + deep - 1)
        for d in reversed(range(1, lights)):
            @pl.when(light + d < lights)
            def _():
                to_light(d, k).start()
        send_x(0, m)

    def join_trans(q):
        owner = lax.rem(z + q, deep) * 2 + x
        to_x(0, q).wait_recv()

        def step(g, carry):
            value = msg[0, owner, g] * xbuf[0, q, g]
            if q:
                comb[0, q - 1, g] = value
            else:
                zbuf[0, 0, g] = value
            return carry

        lax.fori_loop(0, groups, step, 0, unroll=min(4, groups))
        if q:
            to_z(0, q).start()

    def join_color(q):
        owner = lax.rem(z + q, deep) * 2 + x
        to_x(1, q).wait_recv()

        def step(g, carry):
            mine, other = msg[1, owner, g], xbuf[1, q, g]
            value = jnp.where(
                turned(g) == x, mine + msg[0, owner, g] * other, other + xbuf[0, q, g] * mine
            )
            if q:
                comb[1, q - 1, g] = value
            else:
                zbuf[1, 0, g] = value
            return carry

        lax.fori_loop(0, groups, step, 0, unroll=min(4, groups))
        if q:
            to_z(1, q).start()

    def second(k, m, g, lights_in):
        lights_in, colors = list(lights_in), []
        for i in range(n):
            lit, through = [], []
            for v in range(cells):
                d = tile(dens, k, g * n + i, v)
                thin = jnp.exp(d * -light_scale)
                passed = lax.integer_pow(thin, power) if whole_power else jnp.exp(d * -view_scale)
                lit.append(tile(emis, k, g * n + i, v) * (0.2 + lights_in[v]) * (1.0 - passed))
                through.append(passed)
                lights_in[v] = lights_in[v] * thin
            forward, backward = lit[-1], lit[0]
            for v in range(cells - 2, -1, -1):
                forward = lit[v] + through[v] * forward
            for v in range(1, cells):
                backward = lit[v] + through[v] * backward
            colors.append(jnp.where(facing[g * n + i] == 1, backward, forward))
        for o, packed in enumerate(transposed(colors, width, block)):
            msg[1, m * n + o, g] = packed
        return tuple(lights_in)

    incoming[...] = jnp.zeros_like(incoming)
    for k, m in enumerate(visits):
        for d in range(1, lights):
            @pl.when(light >= d)
            def _():
                to_light(d, k).wait_recv()
                incoming[k] += slabs[d - 1, k]
        loads[1][k].wait()
        lights_in = tuple(jnp.exp(incoming[k, v] * -light_scale) for v in range(cells))
        lax.fori_loop(0, groups, functools.partial(second, k, m), lights_in, unroll=2)
        send_x(1, m)
        for q in order[k * per_tile : (k + 1) * per_tile]:
            join_trans(q)
    for q in order:
        join_color(q)
    for q in range(1, deep):
        for t in range(2):
            to_z(t, q).wait_recv()

    def last(g, carry):
        color = [None] * deep
        trans = [None] * deep
        for at in range(deep):
            slot = lax.rem(z + deep - at, deep)
            trans[at], color[at] = zbuf[0, slot, g], zbuf[1, slot, g]
        forward, backward, total = color[-1], color[0], trans[0]
        for at in range(deep - 2, -1, -1):
            forward = color[at] + trans[at] * forward
        for at in range(1, deep):
            backward = color[at] + trans[at] * backward
            total = total * trans[at]
        radiance[g] = jnp.where(turned(g) == 1, backward, forward)
        coverage[g] = total
        return carry

    lax.fori_loop(0, groups, last, 0, unroll=2)

    for d in range(1, lights):
        @pl.when(light + d < lights)
        def _():
            for k in range(tiles):
                to_light(d, k).wait_send()
    for t in range(2):
        for q in range(deep):
            to_x(t, q).wait_send()
            if q:
                to_z(t, q).wait_send()


def shards(density, emission, facing):
    rows, cells, columns = density.shape
    lights, views = lax.axis_size("light"), lax.axis_size("view")
    deep = views // 2
    width = columns // (views * LANES)
    groups = rows * width // SUB
    tiles = columns // (SUB * LANES)

    def linear(a):
        a = a.reshape(rows, cells, columns // LANES, LANES)
        return a.transpose(0, 2, 1, 3).reshape(rows, -1, LANES)

    f32 = jnp.float32
    piece = (groups, SUB, LANES)
    field = (tiles, rows, SUB * cells, LANES)
    radiance, coverage = pl.pallas_call(
        functools.partial(kernel, rows, cells, columns, lights, views),
        out_shape=[jax.ShapeDtypeStruct(piece, f32)] * 2,
        in_specs=[
            pl.BlockSpec(memory_space=pltpu.SMEM),
            pl.BlockSpec(memory_space=pltpu.HBM),
            pl.BlockSpec(memory_space=pltpu.HBM),
        ],
        out_specs=[pl.BlockSpec(memory_space=pltpu.VMEM)] * 2,
        scratch_shapes=[
            pltpu.VMEM(field, f32),
            pltpu.VMEM(field, f32),
            pltpu.VMEM((tiles, cells, SUB, LANES), f32),
            pltpu.VMEM((lights - 1, tiles, cells, SUB, LANES), f32),
            pltpu.VMEM((tiles, cells, SUB, LANES), f32),
            pltpu.VMEM((2, views) + piece, f32),
            pltpu.VMEM((2, deep) + piece, f32),
            pltpu.VMEM((2, deep - 1) + piece, f32),
            pltpu.VMEM((2, deep) + piece, f32),
            pltpu.SemaphoreType.DMA((2, tiles)),
            pltpu.SemaphoreType.DMA((lights - 1, tiles)),
            pltpu.SemaphoreType.DMA((lights - 1, tiles)),
            pltpu.SemaphoreType.DMA((2, deep)),
            pltpu.SemaphoreType.DMA((2, deep)),
            pltpu.SemaphoreType.DMA((2, deep)),
            pltpu.SemaphoreType.DMA((2, deep)),
        ],
        compiler_params=pltpu.CompilerParams(
            collective_id=0, has_side_effects=True, vmem_limit_bytes=52 * 2**20
        ),
    )(facing, linear(density), linear(emission))
    return radiance.reshape(rows, width * LANES), coverage.reshape(rows, width * LANES)


def solution(mesh):
    return jax.shard_map(
        shards,
        mesh=mesh,
        in_specs=(P("light", "view", None), P("light", "view", None), P("light")),
        out_specs=(P("light", "view"), P("light", "view")),
        check_vma=False,
    )
```
